32 devices in a mesh: groups: 2 (over x), gr: 16 (over z, y, core).
Axes of the slice: x: 2, y: 2, z: 4, core: 2. Of those that a mesh axis runs over, the one named last changes fastest.
Arguments:
- embeddings: bfloat16 [131072, 768], P(('groups', 'gr')), parts along dimension 0
- coverage: bfloat16 [131072], P(('groups', 'gr')), parts along dimension 0, may hold values from 0 to 0.5
- cluster: int32 [131072, 1], P(('groups', 'gr')), parts along dimension 0, may hold values from 0 to 31; in each aligned block of 4096 rows (0 to 4095, 4096 to 8191, ...) at most 192 rows name the same one
- candidates: int32 [64, 1024], P(('groups', 'gr')), parts along dimension 0, may hold values from 0 to 3071
Outputs:
- cluster_gains: float32 [64, 1024], P(('groups', 'gr')), parts along dimension 0
- new_coverage: float32 [131072], P(('groups', 'gr')), parts along dimension 0
The draws below stay inside these ranges and needn't reach their ends.
There are 2 independent parts, one for each index of `groups`. The reference program is written for one: setup_inputs(seed, part) draws one part's arguments, and reference() takes and returns one part's arrays. A program takes and returns all parts, laid end to end along the dimension named above; each array names one. Nothing has to cross between parts.
Inputs may be any that keep to these rules, and one draw needn't show every extreme that they name: Every one of the 32 clusters is named by at least one row. Among the 4096 rows of one device (aligned blocks) no cluster is named more than 192 times, a bound that some block reaches.
All inputs are finite; a program needn't handle non-finite values.
Results may differ from the reference program's by a relative error of at most 0.0006.
Values may be sent and summed in bfloat16 or wider, within the bound.
A program may use at most 128 MiB of HBM per device.

```python
import math
import jax
import jax.numpy as jnp
import numpy as np
from jax import lax

D = 768
ROWS_DEV = 4096
CANDS = 1024
CLUSTERS = 32
MOST = 192
SLOTS = 3072
AVERAGE = 2048
ROWS = 65536


def draw_embeddings(key, part):
    key = jax.random.fold_in(key, 11)
    subkeys = jax.random.split(key, 4)
    shared = jax.random.normal(subkeys[0], (D,), jnp.float32)
    loading = 1.5 * jax.random.normal(subkeys[1], (ROWS, 1), jnp.float32)
    jitter = jax.random.normal(subkeys[2], (ROWS, D), jnp.float32)
    spread = jnp.exp(jax.random.uniform(subkeys[3], (ROWS, 1), jnp.float32, -1.2, 1.2))
    return (spread * (loading * shared[None, :] + jitter)).astype(jnp.bfloat16)


def place_ends(result, key, smallest, high):
    index_at = [jax.random.randint(jax.random.fold_in(key, axis), (), 0, length) for axis, length in enumerate(result.shape)]
    longest = result.shape.index(max(result.shape))
    next_to = index_at[:longest] + [(index_at[longest] + 1) % result.shape[longest]] + index_at[longest + 1:]
    return result.at[tuple(index_at)].set(smallest).at[tuple(next_to)].set(high)


def block_levels(own_key, dims, shards, least, largest):
    def one(axis_at, blocks):
        draws = jax.random.uniform(jax.random.fold_in(jax.random.fold_in(own_key, 6), axis_at), (blocks,), jnp.float32, least / len(shards), largest / len(shards))
        return jnp.repeat(jnp.exp(draws), dims[axis_at] // blocks).reshape((-1,) + (1,) * (len(dims) - axis_at - 1))

    factor_of = one(*shards[0])
    for cut in shards[1:]:
        factor_of = factor_of * one(*cut)
    return factor_of


def routed_block(key, own, number, rows, amount, top, reach, skew):
    sequence = jax.random.permutation(key, amount)
    packed, common = load_shares(amount, rows * top, reach, skew, True), load_shares(amount, rows * top, reach, skew, False)
    places = jnp.arange(amount)

    def named(lengths, offset_by):
        used = int((lengths > 0).sum())
        fixed = max(1, used // 4)
        passed = fixed + (places - fixed + offset_by * (used - fixed)) % max(1, amount - fixed)
        return jnp.zeros((amount,), jnp.int32).at[sequence[jnp.where(places < fixed, places, passed)]].set(jnp.asarray(lengths, jnp.int32))

    lengths = jnp.where(number % 4 == 0, named(packed, number // 4), named(common, number - number // 4 - 1))
    mixed = jax.random.permutation(jax.random.fold_in(own, 3), amount)
    donor, receiver = mixed[0:amount // 2 * 2:2], mixed[1:amount // 2 * 2:2]
    room = jnp.minimum(lengths[donor] - 1, reach - lengths[receiver]) // 2
    room = jnp.where((donor == sequence[0]) | (receiver == sequence[0]) | (lengths[receiver] == 0), 0, jnp.maximum(room, 0))
    passed = jax.random.randint(jax.random.fold_in(own, 4), (amount // 2,), 0, 1 << 20) % (room + 1)
    lengths = lengths.at[donor].add(-passed).at[receiver].add(passed)
    items = jnp.searchsorted(jnp.cumsum(lengths), jnp.arange(rows * top), side="right").astype(jnp.int32)
    table = items.reshape(top, rows).T
    table = table[jax.random.permutation(jax.random.fold_in(own, 1), rows)]
    offset_by = jax.random.randint(jax.random.fold_in(own, 2), (rows, 1), 0, top)
    return jnp.take_along_axis(table, (jnp.arange(top)[None, :] + offset_by) % top, axis=1)


def load_shares(amount, total, most, lean, full):
    weights = [(1 << 20) // math.isqrt(standing ** lean) + 1 for standing in range(1, amount + 1)]
    largest = most if full else min(most, max(-(-total // amount), total * weights[0] // sum(weights)))
    least = 1 if total - largest >= amount - 1 else 0
    counts, spare = [largest] + [least] * (amount - 1), total - largest - least * (amount - 1)
    while spare > 0:
        movable = [i for i in range(1, amount) if counts[i] < largest] or [i for i in range(1, amount) if counts[i] < most]
        mass, remaining = sum([weights[i] for i in movable]), spare
        for i in movable:
            extra = min(most - counts[i], max(1, remaining * weights[i] // mass), spare)
            counts[i] = counts[i] + extra
            spare = spare - extra
    return np.array(counts)


def setup_inputs(seed: int = 0, part: int = 0) -> dict:
    keys = jax.random.split(jax.random.key(seed), 5)
    part_splits = jax.random.split(jax.random.fold_in(keys[4], part), 5)
    embeddings = draw_embeddings(jax.random.fold_in(jax.random.fold_in(keys[4], part), 71), part)
    coverage = jnp.clip(0.5 * jax.random.uniform(part_splits[1], (ROWS,), jnp.float32) ** block_levels(part_splits[1], (ROWS,), ((0, 16),), -0.2, 0.2), 0.0, 0.5).astype(jnp.bfloat16)
    cluster_keys = jax.random.split(jax.random.fold_in(part_splits[2], 1), ROWS // ROWS_DEV)
    cluster_turns = jax.random.permutation(jax.random.fold_in(part_splits[2], 3), ROWS // ROWS_DEV)
    cluster = jax.vmap(lambda own, number: routed_block(jax.random.fold_in(part_splits[2], 2), own, number, ROWS_DEV, CLUSTERS, 1, MOST, 2))(cluster_keys, cluster_turns).reshape((ROWS, 1))
    candidates = place_ends(jax.random.randint(part_splits[3], (CLUSTERS, CANDS), 0, SLOTS), jax.random.fold_in(part_splits[3], 1), 0, SLOTS - 1).astype(jnp.int32)
    return {"embeddings": embeddings, "coverage": coverage, "cluster": cluster, "candidates": candidates}


def unit_rows(embeddings):
    widened = embeddings.astype(jnp.float32)
    inverse = lax.rsqrt(lax.optimization_barrier(jnp.sum(widened * widened, axis=1, keepdims=True)) + 1e-06)
    return (widened * inverse).astype(jnp.bfloat16)

def reference(embeddings, coverage, cluster, candidates):
    normed = unit_rows(embeddings)
    labels = cluster[:, 0]
    covered = coverage.astype(jnp.float32)
    slot_line = jnp.arange(SLOTS, dtype=jnp.int32)

    def one_cluster(cluster_no):
        member = labels == cluster_no
        headcount = jnp.sum(member.astype(jnp.int32), dtype=jnp.int32)
        places = jnp.nonzero(member, size=SLOTS, fill_value=0)[0].astype(jnp.int32)
        is_live = slot_line < headcount
        gathered = jnp.take(normed, places, axis=0)
        picked_rank = lax.dynamic_index_in_dim(candidates, cluster_no, 0, keepdims=False) % headcount
        chosen = jnp.take(gathered, picked_rank, axis=0)
        scores = jnp.dot(chosen, gathered.T, preferred_element_type=jnp.float32)
        relief = jnp.maximum(scores - jnp.take(covered, places)[None, :], 0.0)
        gained = lax.optimization_barrier(jnp.sum(jnp.where(is_live[None, :], relief, 0.0), axis=1)) / AVERAGE
        nearest = jnp.where(is_live, lax.optimization_barrier(jnp.max(scores, axis=0)), -2.0)
        return (gained, nearest, places)
    cluster_gains, nearest, places = lax.map(one_cluster, jnp.arange(CLUSTERS, dtype=jnp.int32))
    new_coverage = covered.at[places.reshape(-1)].max(nearest.reshape(-1))
    return (cluster_gains, new_coverage)
```

```python
import functools
import jax
import jax.numpy as jnp
from jax import lax
from jax.experimental import pallas as pl
from jax.experimental.pallas import tpu as pltpu
from jax.sharding import PartitionSpec as P

DEAD = 4.0
F32 = jnp.float32
BF16 = jnp.bfloat16


def unit_rows(embeddings):
    widened = embeddings.astype(F32)
    inverse = lax.rsqrt(jnp.sum(widened * widened, axis=1, keepdims=True) + 1e-06)
    return (widened * inverse).astype(BF16)


def kernel(
    n, owned, cap, average,
    normed, labels, cover, raw,
    gains, fresh,
    target, send, got, send_aux, got_aux, chosen_sum, chosen, relief_sum, near_out, near_in, near_all,
    row_sent, row_here, aux_sent, aux_here, near_sent, near_here,
):
    me = lax.axis_index("gr")
    half = n // 2
    rows = normed.shape[0]
    cands = raw.shape[1]
    clusters = n * owned

    def partner(step):
        same = step // half
        block = (1 - me // half) * (1 - same) + (me // half) * same
        return block * half + (me % half + step % half + same) % half

    barrier = pltpu.get_barrier_semaphore()

    def greet(step, carry):
        pl.semaphore_signal(barrier, inc=1, device_id={"gr": partner(step)}, device_id_type=pl.DeviceIdType.MESH)
        return carry

    lax.fori_loop(0, n - 1, greet, 0)

    tile = 256
    upper = (
        lax.broadcasted_iota(jnp.int32, (tile, tile), 0) < lax.broadcasted_iota(jnp.int32, (tile, tile), 1)
    ).astype(F32).astype(BF16)
    running = jnp.zeros((clusters, 1), F32)
    for block in range(rows // tile):
        span = slice(block * tile, (block + 1) * tile)
        label = labels[:, span]
        hot = (lax.broadcasted_iota(jnp.int32, (clusters, tile), 0) == label).astype(F32)
        before = jnp.dot(hot.astype(BF16), upper, preferred_element_type=F32) + running
        running = running + jnp.sum(hot, axis=1, keepdims=True)
        within = jnp.sum(before * hot, axis=0, keepdims=True)
        target[:, span] = label * cap + within.astype(jnp.int32)

    pl.semaphore_wait(barrier, n - 1)

    def packed(owner, item):
        base = (owner * owned + item) * cap
        hot = (
            lax.broadcasted_iota(jnp.int32, (cap, rows), 0) + base == target[...]
        ).astype(F32).astype(BF16)
        block = jnp.dot(hot, normed[...], preferred_element_type=F32).astype(BF16)
        pair = lax.dot_general(cover[...], hot, (((1,), (1,)), ((), ())), preferred_element_type=F32)
        return block, pair[0:1, :] + DEAD * (1.0 - pair[1:2, :])

    def row_copy(owner, item):
        return pltpu.make_async_remote_copy(
            src_ref=send.at[item, owner], dst_ref=got.at[item, me],
            send_sem=row_sent.at[item, owner], recv_sem=row_here.at[item, me],
            device_id={"gr": owner}, device_id_type=pl.DeviceIdType.MESH,
        )

    def aux_copy(owner, item):
        return pltpu.make_async_remote_copy(
            src_ref=send_aux.at[item, owner], dst_ref=got_aux.at[item, me],
            send_sem=aux_sent.at[item, owner], recv_sem=aux_here.at[item, me],
            device_id={"gr": owner}, device_id_type=pl.DeviceIdType.MESH,
        )

    def near_copy(source, item):
        return pltpu.make_async_remote_copy(
            src_ref=near_out.at[item, source], dst_ref=near_in.at[item, me],
            send_sem=near_sent.at[item, source], recv_sem=near_here.at[item, me],
            device_id={"gr": source}, device_id_type=pl.DeviceIdType.MESH,
        )

    def arrived(ref, sem, source, item):
        pltpu.make_async_remote_copy(
            src_ref=ref.at[item, source], dst_ref=ref.at[item, source],
            send_sem=sem.at[item, source], recv_sem=sem.at[item, source],
            device_id={"gr": source}, device_id_type=pl.DeviceIdType.MESH,
        ).wait_recv()

    def send_item(item, carry):
        def send_one(step, carry):
            owner = partner(step)
            block, aux = packed(owner, item)
            send_aux[item, owner] = aux
            aux_copy(owner, item).start()
            send[item, owner] = block
            row_copy(owner, item).start()
            return carry

        lax.fori_loop(0, n - 1, send_one, 0)
        block, aux = packed(me, item)
        got_aux[item, me] = aux
        got[item, me] = block
        return carry

    lax.fori_loop(0, owned, send_item, 0)

    def score_item(item, carry):
        def await_one(step, carry):
            source = partner(step)
            arrived(got_aux, aux_here, source, item)
            arrived(got, row_here, source, item)
            return carry

        lax.fori_loop(0, n - 1, await_one, 0)

        def count_one(source, total):
            return total + jnp.sum((got_aux[item, source] < 2.0).astype(F32), axis=1, keepdims=True)

        total = lax.fori_loop(0, n, count_one, jnp.zeros((1, 1), F32))
        ranks = raw[item]
        picked = ranks - jnp.floor(ranks / total) * total
        picked = jnp.where(picked < 0.0, picked + total, picked)
        picked = jnp.where(picked >= total, picked - total, picked)
        chosen_sum[...] = jnp.zeros_like(chosen_sum)

        def gather_one(source, start):
            live = got_aux[item, source] < 2.0
            place = lax.broadcasted_iota(jnp.int32, (1, cap), 1).astype(F32) + start
            place = jnp.where(live, place, -1.0)
            hot = (place == picked).astype(F32).astype(BF16)
            chosen_sum[...] += jnp.dot(hot, got[item, source], preferred_element_type=F32)
            return start + jnp.sum(live.astype(F32), axis=1, keepdims=True)

        lax.fori_loop(0, n, gather_one, jnp.zeros((1, 1), F32))
        chosen[...] = chosen_sum[...].astype(BF16)
        relief_sum[...] = jnp.zeros_like(relief_sum)

        def score_one(source, carry):
            scores = lax.dot_general(
                chosen[...], got[item, source], (((1,), (1,)), ((), ())), preferred_element_type=F32
            )
            relief_sum[...] += jnp.maximum(scores - got_aux[item, source], 0.0)
            near_out[item, source] = jnp.max(scores, axis=0, keepdims=True)
            return carry

        lax.fori_loop(0, n, score_one, 0)

        def send_back(step, carry):
            near_copy(partner(step), item).start()
            return carry

        lax.fori_loop(0, n - 1, send_back, 0)
        near_in[item, me] = near_out[item, me]
        gains[item] = jnp.sum(relief_sum[...], axis=1, keepdims=True) / average
        return carry

    lax.fori_loop(0, owned, score_item, 0)

    def finish(step, carry):
        other = partner(step)
        for item in range(owned):
            row_copy(other, item).wait_send()
            aux_copy(other, item).wait_send()
            near_copy(other, item).wait_send()
            arrived(near_in, near_here, other, item)
        return carry

    lax.fori_loop(0, n - 1, finish, 0)

    for owner in range(n):
        for item in range(owned):
            k = owner * owned + item
            near_all[k : k + 1, :] = near_in[item, owner]
    table = near_all[...]
    first = table.astype(BF16)
    rest = table - first.astype(F32)
    second = rest.astype(BF16)
    third = (rest - second.astype(F32)).astype(BF16)
    parts = [part.astype(F32).T.astype(BF16) for part in (first, second, third)]
    for block in range(rows // 512):
        span = slice(block * 512, (block + 1) * 512)
        label = labels[:, span]
        hot = (lax.broadcasted_iota(jnp.int32, (clusters, 512), 0) == label).astype(F32).astype(BF16)
        columns = sum(jnp.dot(part, hot, preferred_element_type=F32) for part in parts)
        slot = target[:, span] - label * cap
        match = lax.broadcasted_iota(jnp.int32, (cap, 512), 0) == slot
        value = jnp.sum(jnp.where(match, columns, 0.0), axis=0, keepdims=True)
        fresh[:, span] = jnp.maximum(cover[0:1, span].astype(F32), value)


def on_device(embeddings, coverage, cluster, candidates):
    n = lax.axis_size("gr")
    owned, cands = candidates.shape
    rows, width = embeddings.shape
    average = rows // owned
    cap = 3 * rows // (2 * owned * n)
    normed = unit_rows(embeddings)
    cover = jnp.concatenate(
        [coverage.reshape(1, rows), jnp.ones((1, rows), BF16), jnp.zeros((14, rows), BF16)], axis=0
    )
    raw = candidates.astype(F32).reshape(owned, cands, 1)
    vmem = pl.BlockSpec(memory_space=pltpu.VMEM)
    dma = pltpu.SemaphoreType.DMA((owned, n))
    gains, fresh = pl.pallas_call(
        functools.partial(kernel, n, owned, cap, average),
        out_shape=(
            jax.ShapeDtypeStruct((owned, cands, 1), F32),
            jax.ShapeDtypeStruct((1, rows), F32),
        ),
        in_specs=[vmem] * 4,
        out_specs=(vmem, vmem),
        scratch_shapes=[
            pltpu.VMEM((1, rows), jnp.int32),
            pltpu.VMEM((owned, n, cap, width), BF16),
            pltpu.VMEM((owned, n, cap, width), BF16),
            pltpu.VMEM((owned, n, 1, cap), F32),
            pltpu.VMEM((owned, n, 1, cap), F32),
            pltpu.VMEM((cands, width), F32),
            pltpu.VMEM((cands, width), BF16),
            pltpu.VMEM((cands, cap), F32),
            pltpu.VMEM((owned, n, 1, cap), F32),
            pltpu.VMEM((owned, n, 1, cap), F32),
            pltpu.VMEM((n * owned, cap), F32),
        ] + [dma] * 6,
        compiler_params=pltpu.CompilerParams(
            collective_id=0, has_side_effects=True, vmem_limit_bytes=60 * 1024 * 1024
        ),
    )(normed, cluster.reshape(1, rows), cover, raw)
    return (gains.reshape(owned, cands), fresh.reshape(rows))


def solution(mesh):
    placed = (
        P(("groups", "gr"), None),
        P(("groups", "gr")),
        P(("groups", "gr"), None),
        P(("groups", "gr"), None),
    )
    return jax.shard_map(
        on_device,
        mesh=mesh,
        in_specs=placed,
        out_specs=(P(("groups", "gr"), None), P(("groups", "gr"))),
        check_vma=False,
    )
```

```python
import functools
import jax
import jax.numpy as jnp
from jax import lax
from jax.experimental import pallas as pl
from jax.experimental.pallas import tpu as pltpu
from jax.sharding import PartitionSpec as P

DEAD = 4.0
F32 = jnp.float32
BF16 = jnp.bfloat16


def kernel(
    n, owned, cap, average,
    embeddings, labels, cover, raw,
    gains, fresh,
    held, target, send_count, got_count, starts, send, got, send_aux, got_aux, chosen_sum, chosen, relief_sum, near_out, near_in, near_all,
    held_in, count_sent, count_here, row_sent, row_here, aux_sent, aux_here, near_sent, near_here,
):
    me = lax.axis_index("gr")
    half = n // 2
    rows = held.shape[0]
    cands = raw.shape[1]
    clusters = n * owned

    load = pltpu.make_async_copy(embeddings, held, held_in)
    load.start()

    def peer(step, sign):
        turn = 1 - step % 2
        last = step // (n - 2)
        across = turn + last - turn * last
        block = (1 - me // half) * across + (me // half) * (1 - across)
        shift = step // 2 + 1 - across
        return block * half + (me % half + half + sign * shift) % half

    def partner(step):
        return peer(step, 1)

    barrier = pltpu.get_barrier_semaphore()

    def greet(step, carry):
        pl.semaphore_signal(barrier, inc=1, device_id={"gr": partner(step)}, device_id_type=pl.DeviceIdType.MESH)
        return carry

    lax.fori_loop(0, n - 1, greet, 0)

    tile = 256
    upper = (
        lax.broadcasted_iota(jnp.int32, (tile, tile), 0) < lax.broadcasted_iota(jnp.int32, (tile, tile), 1)
    ).astype(F32).astype(BF16)
    running = jnp.zeros((clusters, 1), F32)
    for block in range(rows // tile):
        span = slice(block * tile, (block + 1) * tile)
        label = labels[:, span]
        hot = (lax.broadcasted_iota(jnp.int32, (clusters, tile), 0) == label).astype(F32)
        before = jnp.dot(hot.astype(BF16), upper, preferred_element_type=F32) + running
        running = running + jnp.sum(hot, axis=1, keepdims=True)
        within = jnp.sum(before * hot, axis=0, keepdims=True)
        target[:, span] = label * cap + within.astype(jnp.int32)

    for owner in range(n):
        send_count[owner] = jnp.broadcast_to(running[owner * owned : (owner + 1) * owned, :], (owned, 128))
    got_count[me] = send_count[me]

    pl.semaphore_wait(barrier, n - 1)

    def packed(owner, item):
        base = (owner * owned + item) * cap
        hot = (
            lax.broadcasted_iota(jnp.int32, (cap, rows), 0) + base == target[...]
        ).astype(F32).astype(BF16)
        raised = jnp.dot(hot, held[...], preferred_element_type=F32)
        inverse = lax.rsqrt(jnp.sum(raised * raised, axis=1, keepdims=True) + 1e-06)
        block = (raised * inverse).astype(BF16)
        pair = lax.dot_general(cover[...], hot, (((1,), (1,)), ((), ())), preferred_element_type=F32)
        return block, pair[0:1, :] + DEAD * (1.0 - pair[1:2, :])

    def count_copy(owner):
        return pltpu.make_async_remote_copy(
            src_ref=send_count.at[owner], dst_ref=got_count.at[me],
            send_sem=count_sent.at[owner], recv_sem=count_here.at[me],
            device_id={"gr": owner}, device_id_type=pl.DeviceIdType.MESH,
        )

    def row_copy(owner, item):
        return pltpu.make_async_remote_copy(
            src_ref=send.at[item, owner], dst_ref=got.at[item, me],
            send_sem=row_sent.at[item, owner], recv_sem=row_here.at[item, me],
            device_id={"gr": owner}, device_id_type=pl.DeviceIdType.MESH,
        )

    def aux_copy(owner, item):
        return pltpu.make_async_remote_copy(
            src_ref=send_aux.at[item, owner], dst_ref=got_aux.at[item, me],
            send_sem=aux_sent.at[item, owner], recv_sem=aux_here.at[item, me],
            device_id={"gr": owner}, device_id_type=pl.DeviceIdType.MESH,
        )

    def near_copy(source, item):
        return pltpu.make_async_remote_copy(
            src_ref=near_out.at[item, source], dst_ref=near_in.at[item, me],
            send_sem=near_sent.at[item, source], recv_sem=near_here.at[item, me],
            device_id={"gr": source}, device_id_type=pl.DeviceIdType.MESH,
        )

    def arrived(ref, sem, source, item):
        pltpu.make_async_remote_copy(
            src_ref=ref.at[item, source], dst_ref=ref.at[item, source],
            send_sem=sem.at[item, source], recv_sem=sem.at[item, source],
            device_id={"gr": source}, device_id_type=pl.DeviceIdType.MESH,
        ).wait_recv()

    def send_counts(step, carry):
        count_copy(partner(step)).start()
        return carry

    lax.fori_loop(0, n - 1, send_counts, 0)
    load.wait()

    def send_item(item, carry):
        def send_one(step, carry):
            owner = partner(step)
            block, aux = packed(owner, item)
            send_aux[item, owner] = aux
            aux_copy(owner, item).start()
            send[item, owner] = block
            row_copy(owner, item).start()
            return carry

        lax.fori_loop(0, n - 1, send_one, 0)
        block, aux = packed(me, item)
        got_aux[item, me] = aux
        got[item, me] = block
        return carry

    lax.fori_loop(0, owned, send_item, 0)

    def await_counts(step, carry):
        source = partner(step)
        pltpu.make_async_remote_copy(
            src_ref=send_count.at[source], dst_ref=got_count.at[source],
            send_sem=count_sent.at[source], recv_sem=count_here.at[source],
            device_id={"gr": source}, device_id_type=pl.DeviceIdType.MESH,
        ).wait_recv()
        return carry

    lax.fori_loop(0, n - 1, await_counts, 0)
    for item in range(owned):
        ahead = jnp.zeros((1, 128), F32)
        for source in range(n):
            starts[item, source] = ahead
            ahead = ahead + got_count[source][item : item + 1, :]
        starts[item, n] = ahead

    def score_item(item, carry):
        total = starts[item, n][:, 0:1]
        ranks = raw[item]
        picked = ranks - jnp.floor(ranks / total) * total
        picked = jnp.where(picked < 0.0, picked + total, picked)
        picked = jnp.where(picked >= total, picked - total, picked)
        chosen_sum[...] = jnp.zeros_like(chosen_sum)

        def gather(source):
            place = lax.broadcasted_iota(jnp.int32, (1, cap), 1).astype(F32) + starts[item, source][:, 0:1]
            place = jnp.where(got_aux[item, source] < 2.0, place, -1.0)
            hot = (place == picked).astype(F32).astype(BF16)
            chosen_sum[...] += jnp.dot(hot, got[item, source], preferred_element_type=F32)

        gather(me)

        def gather_one(step, carry):
            source = peer(step, -1)
            arrived(got_aux, aux_here, source, item)
            arrived(got, row_here, source, item)
            gather(source)
            return carry

        lax.fori_loop(0, n - 1, gather_one, 0)
        chosen[...] = chosen_sum[...].astype(BF16)
        relief_sum[...] = jnp.zeros_like(relief_sum)

        def score_one(source, carry):
            scores = lax.dot_general(
                chosen[...], got[item, source], (((1,), (1,)), ((), ())), preferred_element_type=F32
            )
            relief_sum[...] += jnp.maximum(scores - got_aux[item, source], 0.0)
            near_out[item, source] = jnp.max(scores, axis=0, keepdims=True)
            return carry

        lax.fori_loop(0, n, score_one, 0)

        def send_back(step, carry):
            near_copy(partner(step), item).start()
            return carry

        lax.fori_loop(0, n - 1, send_back, 0)
        near_in[item, me] = near_out[item, me]
        gains[item] = jnp.sum(relief_sum[...].T, axis=0, keepdims=True) / average
        return carry

    lax.fori_loop(0, owned, score_item, 0)

    def finish(step, carry):
        other = partner(step)
        count_copy(other).wait_send()
        for item in range(owned):
            row_copy(other, item).wait_send()
            aux_copy(other, item).wait_send()
            near_copy(other, item).wait_send()
            arrived(near_in, near_here, other, item)
        return carry

    lax.fori_loop(0, n - 1, finish, 0)

    for owner in range(n):
        for item in range(owned):
            k = owner * owned + item
            near_all[k : k + 1, :] = near_in[item, owner]
    table = near_all[...]
    first = table.astype(BF16)
    rest = table - first.astype(F32)
    second = rest.astype(BF16)
    third = (rest - second.astype(F32)).astype(BF16)
    parts = [part.astype(F32).T.astype(BF16) for part in (first, second, third)]
    for block in range(rows // 512):
        span = slice(block * 512, (block + 1) * 512)
        label = labels[:, span]
        hot = (lax.broadcasted_iota(jnp.int32, (clusters, 512), 0) == label).astype(F32).astype(BF16)
        columns = sum(jnp.dot(part, hot, preferred_element_type=F32) for part in parts)
        slot = target[:, span] - label * cap
        match = lax.broadcasted_iota(jnp.int32, (cap, 512), 0) == slot
        value = jnp.sum(jnp.where(match, columns, 0.0), axis=0, keepdims=True)
        fresh[:, span] = jnp.maximum(cover[0:1, span].astype(F32), value)


def on_device(embeddings, coverage, cluster, candidates):
    n = lax.axis_size("gr")
    owned, cands = candidates.shape
    rows, width = embeddings.shape
    average = rows // owned
    cap = 3 * rows // (2 * owned * n)
    cover = jnp.concatenate(
        [coverage.reshape(1, rows), jnp.ones((1, rows), BF16), jnp.zeros((14, rows), BF16)], axis=0
    )
    raw = candidates.astype(F32).reshape(owned, cands, 1)
    vmem = pl.BlockSpec(memory_space=pltpu.VMEM)
    dma = pltpu.SemaphoreType.DMA((owned, n))
    gains, fresh = pl.pallas_call(
        functools.partial(kernel, n, owned, cap, average),
        out_shape=(
            jax.ShapeDtypeStruct((owned, 1, cands), F32),
            jax.ShapeDtypeStruct((1, rows), F32),
        ),
        in_specs=[pl.BlockSpec(memory_space=pl.ANY)] + [vmem] * 3,
        out_specs=(vmem, vmem),
        scratch_shapes=[
            pltpu.VMEM((rows, width), BF16),
            pltpu.VMEM((1, rows), jnp.int32),
            pltpu.VMEM((n, owned, 128), F32),
            pltpu.VMEM((n, owned, 128), F32),
            pltpu.VMEM((owned, n + 1, 1, 128), F32),
            pltpu.VMEM((owned, n, cap, width), BF16),
            pltpu.VMEM((owned, n, cap, width), BF16),
            pltpu.VMEM((owned, n, 1, cap), F32),
            pltpu.VMEM((owned, n, 1, cap), F32),
            pltpu.VMEM((cands, width), F32),
            pltpu.VMEM((cands, width), BF16),
            pltpu.VMEM((cands, cap), F32),
            pltpu.VMEM((owned, n, 1, cap), F32),
            pltpu.VMEM((owned, n, 1, cap), F32),
            pltpu.VMEM((n * owned, cap), F32),
        ] + [pltpu.SemaphoreType.DMA] + [pltpu.SemaphoreType.DMA((n,))] * 2 + [dma] * 6,
        compiler_params=pltpu.CompilerParams(
            collective_id=0, has_side_effects=True, vmem_limit_bytes=60 * 1024 * 1024
        ),
    )(embeddings, cluster.reshape(1, rows), cover, raw)
    return (gains.reshape(owned, cands), fresh.reshape(rows))


def solution(mesh):
    placed = (
        P(("groups", "gr"), None),
        P(("groups", "gr")),
        P(("groups", "gr"), None),
        P(("groups", "gr"), None),
    )
    return jax.shard_map(
        on_device,
        mesh=mesh,
        in_specs=placed,
        out_specs=(P(("groups", "gr"), None), P(("groups", "gr"))),
        check_vma=False,
    )
```

```python
import functools
import jax
import jax.numpy as jnp
from jax import lax
from jax.experimental import pallas as pl
from jax.experimental.pallas import tpu as pltpu
from jax.sharding import PartitionSpec as P

DEAD = 4.0
F32 = jnp.float32
BF16 = jnp.bfloat16


def kernel(
    n, owned, cap, average,
    embeddings, labels, cover, raw,
    gains, fresh,
    held, target, send_count, got_count, starts, send, got, send_aux, got_aux, chosen_sum, chosen, relief_sum, near_out, near_in, near_all,
    held_in, count_sent, count_here, row_sent, row_here, aux_sent, aux_here, near_sent, near_here,
):
    me = lax.axis_index("gr")
    half = n // 2
    rows = held.shape[0]
    cands = raw.shape[1]
    clusters = n * owned
    fold = relief_sum.shape[1] // cap

    load = pltpu.make_async_copy(embeddings, held, held_in)
    load.start()

    def peer(step, sign):
        turn = 1 - step % 2
        last = step // (n - 2)
        across = turn + last - turn * last
        block = (1 - me // half) * across + (me // half) * (1 - across)
        shift = step // 2 + 1 - across
        return block * half + (me % half + half + sign * shift) % half

    def partner(step):
        return peer(step, 1)

    barrier = pltpu.get_barrier_semaphore()

    def greet(step, carry):
        pl.semaphore_signal(barrier, inc=1, device_id={"gr": partner(step)}, device_id_type=pl.DeviceIdType.MESH)
        return carry

    lax.fori_loop(0, n - 1, greet, 0)

    tile = 256
    upper = (
        lax.broadcasted_iota(jnp.int32, (tile, tile), 0) < lax.broadcasted_iota(jnp.int32, (tile, tile), 1)
    ).astype(F32).astype(BF16)
    running = jnp.zeros((clusters, 1), F32)
    for block in range(rows // tile):
        span = slice(block * tile, (block + 1) * tile)
        label = labels[:, span]
        hot = (lax.broadcasted_iota(jnp.int32, (clusters, tile), 0) == label).astype(F32)
        before = jnp.dot(hot.astype(BF16), upper, preferred_element_type=F32) + running
        running = running + jnp.sum(hot, axis=1, keepdims=True)
        within = jnp.sum(before * hot, axis=0, keepdims=True)
        target[:, span] = label * cap + within.astype(jnp.int32)

    for owner in range(n):
        send_count[owner] = jnp.broadcast_to(running[owner * owned : (owner + 1) * owned, :], (owned, 128))
    got_count[me] = send_count[me]

    pl.semaphore_wait(barrier, n - 1)

    def packed(owner, item):
        base = (owner * owned + item) * cap
        hot = (
            lax.broadcasted_iota(jnp.int32, (cap, rows), 0) + base == target[...]
        ).astype(F32).astype(BF16)
        raised = jnp.dot(hot, held[...], preferred_element_type=F32)
        inverse = lax.rsqrt(jnp.sum(raised * raised, axis=1, keepdims=True) + 1e-06)
        block = (raised * inverse).astype(BF16)
        pair = lax.dot_general(cover[...], hot, (((1,), (1,)), ((), ())), preferred_element_type=F32)
        return block, pair[0:1, :] + DEAD * (1.0 - pair[1:2, :])

    def count_copy(owner):
        return pltpu.make_async_remote_copy(
            src_ref=send_count.at[owner], dst_ref=got_count.at[me],
            send_sem=count_sent.at[owner], recv_sem=count_here.at[me],
            device_id={"gr": owner}, device_id_type=pl.DeviceIdType.MESH,
        )

    def row_copy(owner, item):
        return pltpu.make_async_remote_copy(
            src_ref=send.at[item, owner], dst_ref=got.at[item, me],
            send_sem=row_sent.at[item, owner], recv_sem=row_here.at[item, me],
            device_id={"gr": owner}, device_id_type=pl.DeviceIdType.MESH,
        )

    def aux_copy(owner, item):
        return pltpu.make_async_remote_copy(
            src_ref=send_aux.at[item, owner], dst_ref=got_aux.at[item, me],
            send_sem=aux_sent.at[item, owner], recv_sem=aux_here.at[item, me],
            device_id={"gr": owner}, device_id_type=pl.DeviceIdType.MESH,
        )

    def near_copy(source, item):
        return pltpu.make_async_remote_copy(
            src_ref=near_out.at[item, source], dst_ref=near_in.at[item, me],
            send_sem=near_sent.at[item, source], recv_sem=near_here.at[item, me],
            device_id={"gr": source}, device_id_type=pl.DeviceIdType.MESH,
        )

    def arrived(ref, sem, source, item):
        pltpu.make_async_remote_copy(
            src_ref=ref.at[item, source], dst_ref=ref.at[item, source],
            send_sem=sem.at[item, source], recv_sem=sem.at[item, source],
            device_id={"gr": source}, device_id_type=pl.DeviceIdType.MESH,
        ).wait_recv()

    def send_counts(step, carry):
        count_copy(partner(step)).start()
        return carry

    lax.fori_loop(0, n - 1, send_counts, 0)
    load.wait()

    def send_item(item, carry):
        def send_one(step, carry):
            owner = partner(step)
            block, aux = packed(owner, item)
            send_aux[item, owner] = aux
            aux_copy(owner, item).start()
            send[item, owner] = block
            row_copy(owner, item).start()
            return carry

        lax.fori_loop(0, n - 1, send_one, 0)
        block, aux = packed(me, item)
        got_aux[item, me] = aux
        got[item, me] = block
        return carry

    lax.fori_loop(0, owned, send_item, 0)

    def await_counts(step, carry):
        source = partner(step)
        pltpu.make_async_remote_copy(
            src_ref=send_count.at[source], dst_ref=got_count.at[source],
            send_sem=count_sent.at[source], recv_sem=count_here.at[source],
            device_id={"gr": source}, device_id_type=pl.DeviceIdType.MESH,
        ).wait_recv()
        return carry

    lax.fori_loop(0, n - 1, await_counts, 0)
    for item in range(owned):
        ahead = jnp.zeros((1, 128), F32)
        for source in range(n):
            starts[item, source] = ahead
            ahead = ahead + got_count[source][item : item + 1, :]
        starts[item, n] = ahead

    def score_item(item, carry):
        total = starts[item, n][:, 0:1]
        ranks = raw[item]
        picked = ranks - jnp.floor(ranks / total) * total
        picked = jnp.where(picked < 0.0, picked + total, picked)
        picked = jnp.where(picked >= total, picked - total, picked)
        chosen_sum[...] = jnp.zeros_like(chosen_sum)

        def gather(source):
            place = lax.broadcasted_iota(jnp.int32, (1, cap), 1).astype(F32) + starts[item, source][:, 0:1]
            place = jnp.where(got_aux[item, source] < 2.0, place, -1.0)
            hot = (place == picked).astype(F32).astype(BF16)
            chosen_sum[...] += jnp.dot(hot, got[item, source], preferred_element_type=F32)

        gather(me)

        def gather_one(step, carry):
            source = peer(step, -1)
            arrived(got_aux, aux_here, source, item)
            arrived(got, row_here, source, item)
            gather(source)
            return carry

        lax.fori_loop(0, n - 1, gather_one, 0)
        chosen[...] = chosen_sum[...].astype(BF16)
        relief_sum[...] = jnp.zeros_like(relief_sum)

        def score_one(part, carry):
            first = part * fold
            scores = lax.dot_general(
                chosen[...],
                got[item, pl.ds(first, fold)].reshape(fold * cap, chosen.shape[1]),
                (((1,), (1,)), ((), ())), preferred_element_type=F32,
            )
            aux = jnp.concatenate([got_aux[item, first + place] for place in range(fold)], axis=1)
            relief_sum[...] += jnp.maximum(scores - aux, 0.0)
            near = jnp.max(scores, axis=0, keepdims=True)
            for place in range(fold):
                near_out[item, first + place] = near[:, place * cap : (place + 1) * cap]
            return carry

        lax.fori_loop(0, n // fold, score_one, 0)

        def send_back(step, carry):
            near_copy(partner(step), item).start()
            return carry

        lax.fori_loop(0, n - 1, send_back, 0)
        near_in[item, me] = near_out[item, me]
        gains[item] = jnp.sum(relief_sum[...].T, axis=0, keepdims=True) / average
        return carry

    lax.fori_loop(0, owned, score_item, 0)

    def finish(step, carry):
        other = partner(step)
        count_copy(other).wait_send()
        for item in range(owned):
            row_copy(other, item).wait_send()
            aux_copy(other, item).wait_send()
            near_copy(other, item).wait_send()
            arrived(near_in, near_here, other, item)
        return carry

    lax.fori_loop(0, n - 1, finish, 0)

    for owner in range(n):
        for item in range(owned):
            k = owner * owned + item
            near_all[k : k + 1, :] = near_in[item, owner]
    table = near_all[...]
    first = table.astype(BF16)
    rest = table - first.astype(F32)
    second = rest.astype(BF16)
    third = (rest - second.astype(F32)).astype(BF16)
    parts = [part.astype(F32).T.astype(BF16) for part in (first, second, third)]
    for block in range(rows // 512):
        span = slice(block * 512, (block + 1) * 512)
        label = labels[:, span]
        hot = (lax.broadcasted_iota(jnp.int32, (clusters, 512), 0) == label).astype(F32).astype(BF16)
        columns = sum(jnp.dot(part, hot, preferred_element_type=F32) for part in parts)
        slot = target[:, span] - label * cap
        match = lax.broadcasted_iota(jnp.int32, (cap, 512), 0) == slot
        value = jnp.sum(jnp.where(match, columns, 0.0), axis=0, keepdims=True)
        fresh[:, span] = jnp.maximum(cover[0:1, span].astype(F32), value)


def on_device(embeddings, coverage, cluster, candidates):
    n = lax.axis_size("gr")
    owned, cands = candidates.shape
    rows, width = embeddings.shape
    average = rows // owned
    cap = 3 * rows // (2 * owned * n)
    cover = jnp.concatenate(
        [coverage.reshape(1, rows), jnp.ones((1, rows), BF16), jnp.zeros((14, rows), BF16)], axis=0
    )
    raw = candidates.astype(F32).reshape(owned, cands, 1)
    vmem = pl.BlockSpec(memory_space=pltpu.VMEM)
    dma = pltpu.SemaphoreType.DMA((owned, n))
    gains, fresh = pl.pallas_call(
        functools.partial(kernel, n, owned, cap, average),
        out_shape=(
            jax.ShapeDtypeStruct((owned, 1, cands), F32),
            jax.ShapeDtypeStruct((1, rows), F32),
        ),
        in_specs=[pl.BlockSpec(memory_space=pl.ANY)] + [vmem] * 3,
        out_specs=(vmem, vmem),
        scratch_shapes=[
            pltpu.VMEM((rows, width), BF16),
            pltpu.VMEM((1, rows), jnp.int32),
            pltpu.VMEM((n, owned, 128), F32),
            pltpu.VMEM((n, owned, 128), F32),
            pltpu.VMEM((owned, n + 1, 1, 128), F32),
            pltpu.VMEM((owned, n, cap, width), BF16),
            pltpu.VMEM((owned, n, cap, width), BF16),
            pltpu.VMEM((owned, n, 1, cap), F32),
            pltpu.VMEM((owned, n, 1, cap), F32),
            pltpu.VMEM((cands, width), F32),
            pltpu.VMEM((cands, width), BF16),
            pltpu.VMEM((cands, 4 * cap), F32),
            pltpu.VMEM((owned, n, 1, cap), F32),
            pltpu.VMEM((owned, n, 1, cap), F32),
            pltpu.VMEM((n * owned, cap), F32),
        ] + [pltpu.SemaphoreType.DMA] + [pltpu.SemaphoreType.DMA((n,))] * 2 + [dma] * 6,
        compiler_params=pltpu.CompilerParams(
            collective_id=0, has_side_effects=True, vmem_limit_bytes=60 * 1024 * 1024
        ),
    )(embeddings, cluster.reshape(1, rows), cover, raw)
    return (gains.reshape(owned, cands), fresh.reshape(rows))


def solution(mesh):
    placed = (
        P(("groups", "gr"), None),
        P(("groups", "gr")),
        P(("groups", "gr"), None),
        P(("groups", "gr"), None),
    )
    return jax.shard_map(
        on_device,
        mesh=mesh,
        in_specs=placed,
        out_specs=(P(("groups", "gr"), None), P(("groups", "gr"))),
        check_vma=False,
    )
```

```python
import functools
import jax
import jax.numpy as jnp
from jax import lax
from jax.experimental import pallas as pl
from jax.experimental.pallas import tpu as pltpu
from jax.sharding import PartitionSpec as P

DEAD = 4.0
F32 = jnp.float32
BF16 = jnp.bfloat16


def kernel(
    n, owned, cap, average,
    embeddings, labels, cover, raw,
    gains, fresh,
    held, target, send_count, got_count, starts, send, got, send_aux, got_aux, chosen_sum, chosen, relief_sum, near_out, near_in, near_all,
    held_in, count_sent, count_here, row_sent, row_here, aux_sent, aux_here, near_sent, near_here,
):
    me = lax.axis_index("gr")
    half = n // 2
    rows = held.shape[0]
    cands = raw.shape[1]
    clusters = n * owned
    fold = relief_sum.shape[1] // cap

    load = pltpu.make_async_copy(embeddings, held, held_in)
    load.start()

    def peer(step, sign):
        turn = 1 - step % 2
        last = step // (n - 2)
        across = turn + last - turn * last
        block = (1 - me // half) * across + (me // half) * (1 - across)
        shift = step // 2 + 1 - across
        return block * half + (me % half + half + sign * shift) % half

    def partner(step):
        return peer(step, 1)

    barrier = pltpu.get_barrier_semaphore()

    def greet(step, carry):
        pl.semaphore_signal(barrier, inc=1, device_id={"gr": partner(step)}, device_id_type=pl.DeviceIdType.MESH)
        return carry

    lax.fori_loop(0, n - 1, greet, 0)

    tile = 256
    upper = (
        lax.broadcasted_iota(jnp.int32, (tile, tile), 0) < lax.broadcasted_iota(jnp.int32, (tile, tile), 1)
    ).astype(F32).astype(BF16)
    running = jnp.zeros((clusters, 1), F32)
    for block in range(rows // tile):
        span = slice(block * tile, (block + 1) * tile)
        label = labels[:, span]
        hot = (lax.broadcasted_iota(jnp.int32, (clusters, tile), 0) == label).astype(F32)
        before = jnp.dot(hot.astype(BF16), upper, preferred_element_type=F32) + running
        running = running + jnp.sum(hot, axis=1, keepdims=True)
        within = jnp.sum(before * hot, axis=0, keepdims=True)
        target[:, span] = label * cap + within.astype(jnp.int32)

    for owner in range(n):
        send_count[owner] = jnp.broadcast_to(running[owner * owned : (owner + 1) * owned, :], (owned, 128))
    got_count[me] = send_count[me]

    pl.semaphore_wait(barrier, n - 1)

    def packed(owner, item):
        base = (owner * owned + item) * cap
        hot = (
            lax.broadcasted_iota(jnp.int32, (cap, rows), 0) + base == target[...]
        ).astype(F32).astype(BF16)
        raised = jnp.dot(hot, held[...], preferred_element_type=F32)
        inverse = lax.rsqrt(jnp.sum(raised * raised, axis=1, keepdims=True) + 1e-06)
        block = (raised * inverse).astype(BF16)
        pair = lax.dot_general(cover[...], hot, (((1,), (1,)), ((), ())), preferred_element_type=F32)
        return block, pair[0:1, :] + DEAD * (1.0 - pair[1:2, :])

    def count_copy(owner):
        return pltpu.make_async_remote_copy(
            src_ref=send_count.at[owner], dst_ref=got_count.at[me],
            send_sem=count_sent.at[owner], recv_sem=count_here.at[me],
            device_id={"gr": owner}, device_id_type=pl.DeviceIdType.MESH,
        )

    def row_copy(owner, item):
        return pltpu.make_async_remote_copy(
            src_ref=send.at[item, owner], dst_ref=got.at[item, me],
            send_sem=row_sent.at[item, owner], recv_sem=row_here.at[item, me],
            device_id={"gr": owner}, device_id_type=pl.DeviceIdType.MESH,
        )

    def aux_copy(owner, item):
        return pltpu.make_async_remote_copy(
            src_ref=send_aux.at[item, owner], dst_ref=got_aux.at[item, me],
            send_sem=aux_sent.at[item, owner], recv_sem=aux_here.at[item, me],
            device_id={"gr": owner}, device_id_type=pl.DeviceIdType.MESH,
        )

    def near_copy(source, item):
        return pltpu.make_async_remote_copy(
            src_ref=near_out.at[item, source], dst_ref=near_in.at[item, me],
            send_sem=near_sent.at[item, source], recv_sem=near_here.at[item, me],
            device_id={"gr": source}, device_id_type=pl.DeviceIdType.MESH,
        )

    def arrived(ref, sem, source, item):
        pltpu.make_async_remote_copy(
            src_ref=ref.at[item, source], dst_ref=ref.at[item, source],
            send_sem=sem.at[item, source], recv_sem=sem.at[item, source],
            device_id={"gr": source}, device_id_type=pl.DeviceIdType.MESH,
        ).wait_recv()

    def send_counts(step, carry):
        count_copy(partner(step)).start()
        return carry

    lax.fori_loop(0, n - 1, send_counts, 0)
    load.wait()

    def send_item(item, carry):
        def send_one(step, carry):
            owner = partner(step)
            block, aux = packed(owner, item)
            send_aux[item, owner] = aux
            aux_copy(owner, item).start()
            send[item, owner] = block
            row_copy(owner, item).start()
            return carry

        lax.fori_loop(0, n - 1, send_one, 0)
        block, aux = packed(me, item)
        got_aux[item, me] = aux
        got[item, me] = block
        return carry

    lax.fori_loop(0, owned, send_item, 0)

    def await_counts(step, carry):
        source = partner(step)
        pltpu.make_async_remote_copy(
            src_ref=send_count.at[source], dst_ref=got_count.at[source],
            send_sem=count_sent.at[source], recv_sem=count_here.at[source],
            device_id={"gr": source}, device_id_type=pl.DeviceIdType.MESH,
        ).wait_recv()
        return carry

    lax.fori_loop(0, n - 1, await_counts, 0)
    for item in range(owned):
        ahead = jnp.zeros((1, 128), F32)
        for source in range(n):
            starts[item, source] = ahead
            ahead = ahead + got_count[source][item : item + 1, :]
        starts[item, n] = ahead

    def score_item(item, carry):
        total = starts[item, n][:, 0:1]
        ranks = raw[item]
        picked = ranks - jnp.floor(ranks / total) * total
        picked = jnp.where(picked < 0.0, picked + total, picked)
        picked = jnp.where(picked >= total, picked - total, picked)
        chosen_sum[...] = jnp.zeros_like(chosen_sum)

        def gather(source):
            place = lax.broadcasted_iota(jnp.int32, (1, cap), 1).astype(F32) + starts[item, source][:, 0:1]
            place = jnp.where(got_aux[item, source] < 2.0, place, -1.0)
            hot = (place == picked).astype(F32).astype(BF16)
            chosen_sum[...] += jnp.dot(hot, got[item, source], preferred_element_type=F32)

        gather(me)

        def gather_one(step, carry):
            source = peer(step, -1)
            arrived(got_aux, aux_here, source, item)
            arrived(got, row_here, source, item)
            gather(source)
            return carry

        lax.fori_loop(0, n - 1, gather_one, 0)
        chosen[...] = chosen_sum[...].astype(BF16)
        relief_sum[...] = jnp.zeros_like(relief_sum)

        def score_one(part, carry):
            first = part * fold
            scores = lax.dot_general(
                chosen[...],
                got[item, pl.ds(first, fold)].reshape(fold * cap, chosen.shape[1]),
                (((1,), (1,)), ((), ())), preferred_element_type=F32,
            )
            aux = jnp.concatenate([got_aux[item, first + place] for place in range(fold)], axis=1)
            relief_sum[...] += jnp.maximum(scores - aux, 0.0)
            near = jnp.max(scores, axis=0, keepdims=True)
            for place in range(fold):
                source = first + place
                near_out[item, source] = near[:, place * cap : (place + 1) * cap]

                @pl.when(source != me)
                def _():
                    near_copy(source, item).start()

            return carry

        lax.fori_loop(0, n // fold, score_one, 0)

        near_in[item, me] = near_out[item, me]
        lanes = 128 if fold * cap % 128 == 0 else fold * cap
        folded = sum(relief_sum[:, at : at + lanes] for at in range(0, fold * cap, lanes))
        gains[item] = jnp.sum(folded.T, axis=0, keepdims=True) / average
        return carry

    lax.fori_loop(0, owned, score_item, 0)

    def finish(step, carry):
        other = partner(step)
        count_copy(other).wait_send()
        for item in range(owned):
            row_copy(other, item).wait_send()
            aux_copy(other, item).wait_send()
            near_copy(other, item).wait_send()
            arrived(near_in, near_here, other, item)
        return carry

    lax.fori_loop(0, n - 1, finish, 0)

    for owner in range(n):
        for item in range(owned):
            k = owner * owned + item
            near_all[k : k + 1, :] = near_in[item, owner]
    table = near_all[...]
    first = table.astype(BF16)
    rest = table - first.astype(F32)
    second = rest.astype(BF16)
    third = (rest - second.astype(F32)).astype(BF16)
    parts = [part.astype(F32).T.astype(BF16) for part in (first, second, third)]
    for block in range(rows // 512):
        span = slice(block * 512, (block + 1) * 512)
        label = labels[:, span]
        hot = (lax.broadcasted_iota(jnp.int32, (clusters, 512), 0) == label).astype(F32).astype(BF16)
        columns = sum(jnp.dot(part, hot, preferred_element_type=F32) for part in parts)
        slot = target[:, span] - label * cap
        match = lax.broadcasted_iota(jnp.int32, (cap, 512), 0) == slot
        value = jnp.sum(jnp.where(match, columns, 0.0), axis=0, keepdims=True)
        fresh[:, span] = jnp.maximum(cover[0:1, span].astype(F32), value)


def on_device(embeddings, coverage, cluster, candidates):
    n = lax.axis_size("gr")
    owned, cands = candidates.shape
    rows, width = embeddings.shape
    average = rows // owned
    cap = 3 * rows // (2 * owned * n)
    cover = jnp.concatenate(
        [coverage.reshape(1, rows), jnp.ones((1, rows), BF16), jnp.zeros((14, rows), BF16)], axis=0
    )
    raw = candidates.astype(F32).reshape(owned, cands, 1)
    vmem = pl.BlockSpec(memory_space=pltpu.VMEM)
    dma = pltpu.SemaphoreType.DMA((owned, n))
    gains, fresh = pl.pallas_call(
        functools.partial(kernel, n, owned, cap, average),
        out_shape=(
            jax.ShapeDtypeStruct((owned, 1, cands), F32),
            jax.ShapeDtypeStruct((1, rows), F32),
        ),
        in_specs=[pl.BlockSpec(memory_space=pl.ANY)] + [vmem] * 3,
        out_specs=(vmem, vmem),
        scratch_shapes=[
            pltpu.VMEM((rows, width), BF16),
            pltpu.VMEM((1, rows), jnp.int32),
            pltpu.VMEM((n, owned, 128), F32),
            pltpu.VMEM((n, owned, 128), F32),
            pltpu.VMEM((owned, n + 1, 1, 128), F32),
            pltpu.VMEM((owned, n, cap, width), BF16),
            pltpu.VMEM((owned, n, cap, width), BF16),
            pltpu.VMEM((owned, n, 1, cap), F32),
            pltpu.VMEM((owned, n, 1, cap), F32),
            pltpu.VMEM((cands, width), F32),
            pltpu.VMEM((cands, width), BF16),
            pltpu.VMEM((cands, 4 * cap), F32),
            pltpu.VMEM((owned, n, 1, cap), F32),
            pltpu.VMEM((owned, n, 1, cap), F32),
            pltpu.VMEM((n * owned, cap), F32),
        ] + [pltpu.SemaphoreType.DMA] + [pltpu.SemaphoreType.DMA((n,))] * 2 + [dma] * 6,
        compiler_params=pltpu.CompilerParams(
            collective_id=0, has_side_effects=True, vmem_limit_bytes=60 * 1024 * 1024
        ),
    )(embeddings, cluster.reshape(1, rows), cover, raw)
    return (gains.reshape(owned, cands), fresh.reshape(rows))


def solution(mesh):
    placed = (
        P(("groups", "gr"), None),
        P(("groups", "gr")),
        P(("groups", "gr"), None),
        P(("groups", "gr"), None),
    )
    return jax.shard_map(
        on_device,
        mesh=mesh,
        in_specs=placed,
        out_specs=(P(("groups", "gr"), None), P(("groups", "gr"))),
        check_vma=False,
    )
```
